512 devices in a mesh: win: 32 (over x, y), seq: 16 (over z, core).
Axes of the slice: x: 4, y: 8, z: 8, core: 2. Of those that a mesh axis runs over, the one named last changes fastest.
Arguments:
- img_query: bfloat16 [128, 64, 2048], P('win', 'seq'), may hold values from -5 to 5, as said below
- img_key: bfloat16 [128, 64, 2048], P('win', 'seq'), may hold values from -5 to 5
- img_value: bfloat16 [128, 64, 2048], P('win', 'seq'), may hold values from -70 to 70
- text_kv: bfloat16 [2, 2, 512, 2048], P(None, None, None, 'seq'), may hold values from -6 to 6
- vel_weight: bfloat16 [2048, 64], P('seq'), may hold values from -0.125 to 0.125
- window_px: int32 [32], replicated, may hold values from 0 to 2032, as said below
Outputs:
- guided: float32 [128, 64, 64], P('win', 'seq')
The draws below stay inside these ranges and needn't reach their ends.
Inputs may be any that keep to these rules, and one draw needn't show every extreme that they name: `img_query`: queries and keys lie within the range. `window_px`: multiples of 16. Taken in increasing order, the k-th offset lies in [16 k * 4, 16 (k + 1) * 4) for k = 0 to 31; the smallest is 0 and the largest 16 (127).
All inputs are finite; a program needn't handle non-finite values.
Results may differ from the reference program's by a relative error of at most 0.0031.
Values may be sent and summed in bfloat16 or wider, within the bound.
A program may use at most 64 MiB of HBM per device.

```python
import math
import jax
import jax.numpy as jnp
from jax import lax

HD = 128
HEADS = 16
LAT = 64
TXT = 512
WIN_ROWS = 32
WIN_COLS = 64
ROWS_DEV = 4
ROWS = 128
WINDOWS = 32


def draw_img_query(key, part):
    key = jax.random.fold_in(key, 11)
    return (1.6 * jax.random.truncated_normal(key, -3.0, 3.0, (ROWS, WIN_COLS, HEADS * HD), jnp.float32)).astype(jnp.bfloat16)


def draw_img_key(key, part):
    key = jax.random.fold_in(key, 12)
    return (1.6 * jax.random.truncated_normal(key, -3.0, 3.0, (ROWS, WIN_COLS, HEADS * HD), jnp.float32)).astype(jnp.bfloat16)


def draw_img_value(key, part):
    key = jax.random.fold_in(key, 13)
    key_scale, key_base = jax.random.split(key, 2)
    rise_rows = 1.0 + 2.0 * jnp.arange(ROWS, dtype=jnp.float32) / ROWS
    row_scale = jnp.exp(jax.random.uniform(key_scale, (ROWS,), jnp.float32, 0.0, 1.098612))
    base_vals = jax.random.truncated_normal(key_base, -4.0, 4.0, (ROWS, WIN_COLS, HEADS * HD), jnp.float32)
    return ((row_scale * rise_rows)[:, None, None] * base_vals).astype(jnp.bfloat16)


def draw_text_kv(key, part):
    key = jax.random.fold_in(key, 15)
    return (2.0 * jax.random.truncated_normal(key, -3.0, 3.0, (2, 2, TXT, HEADS * HD), jnp.float32)).astype(jnp.bfloat16)


def draw_window_px(key, part):
    key = jax.random.fold_in(key, 14)
    key_jitter, key_order = jax.random.split(key)
    slot_ids = jnp.arange(WINDOWS, dtype=jnp.int32)
    jitter = jax.random.randint(key_jitter, (WINDOWS,), 0, ROWS_DEV, dtype=jnp.int32)
    jitter = jnp.where(slot_ids == 0, 0, jnp.where(slot_ids == WINDOWS - 1, ROWS_DEV - 1, jitter))
    starts = slot_ids * ROWS_DEV + jitter
    shuffled = jax.random.permutation(key_order, WINDOWS)
    return (16 * starts[shuffled]).astype(jnp.int32)


def block_scale(stream_key, dims, cuts, low, largest):
    gain, own = 1.0, jax.random.fold_in(stream_key, 6)
    for dim, parts in cuts:
        heights = jnp.exp(jax.random.uniform(jax.random.fold_in(own, dim), (parts,), jnp.float32, low / len(cuts), largest / len(cuts)))
        gain = gain * jnp.repeat(heights, dims[dim] // parts).reshape([-1 if axis == dim else 1 for axis in range(len(dims))])
    return gain


def normal_values(key, extent, width, limit, cuts=(), held_as=jnp.bfloat16):
    level = block_scale(key, extent, cuts, -0.22, 0.18) if cuts else 1.0
    array = jax.random.normal(key, extent, jnp.float32) * width * level
    return jnp.minimum(jnp.maximum(array, -limit), limit).astype(held_as)


def setup_inputs(seed: int = 0) -> dict:
    splits = jax.random.split(jax.random.key(seed), 7)
    return {
        "img_query": draw_img_query(jax.random.fold_in(splits[6], 71), 0),
        "img_key": draw_img_key(jax.random.fold_in(splits[6], 71), 0),
        "img_value": draw_img_value(jax.random.fold_in(splits[6], 71), 0),
        "text_kv": draw_text_kv(jax.random.fold_in(splits[6], 71), 0),
        "vel_weight": normal_values(splits[4], (HEADS * HD, LAT), (HEADS * HD) ** -0.5, 0.125, ((0, 16),)),
        "window_px": draw_window_px(jax.random.fold_in(splits[6], 71), 0),
    }


clip_rms = 0.3
guide_scale = 5.0
tiny = 1e-06

def attend_head(queries, key_rows, value_rows):
    inv_root = 1.0 / math.sqrt(queries.shape[-1])
    scores = jnp.dot(queries.astype(jnp.float32), key_rows.astype(jnp.float32).T, preferred_element_type=jnp.float32) * inv_root
    weights = jax.nn.softmax(scores, axis=-1).astype(jnp.bfloat16)
    return jnp.dot(weights.astype(jnp.float32), value_rows.astype(jnp.float32), preferred_element_type=jnp.float32).astype(jnp.bfloat16)

def window_velocity(start, img_query, img_key, img_value, text_kv, vel_weight):
    rows_idx = jnp.mod(start + jnp.arange(WIN_ROWS, dtype=jnp.int32), ROWS).astype(jnp.int32)
    tok_count = WIN_ROWS * WIN_COLS
    window_slabs = [jnp.moveaxis(jnp.take(canvas_part, rows_idx, axis=0).reshape(tok_count, HEADS, HD), 1, 0) for canvas_part in (img_query, img_key, img_value)]
    text_heads = jnp.moveaxis(text_kv.reshape(2, 2, TXT, HEADS, HD), 3, 0)

    def per_head(packed):
        queries, key_rows, value_rows, text_pair = packed
        branch_outs = []
        for branch in range(2):
            keys_all = jnp.concatenate([key_rows, text_pair[branch, 0]], axis=0)
            values_all = jnp.concatenate([value_rows, text_pair[branch, 1]], axis=0)
            branch_outs.append(attend_head(queries, keys_all, values_all))
        return jnp.stack(branch_outs, axis=1)
    attn_out = lax.map(per_head, (window_slabs[0], window_slabs[1], window_slabs[2], text_heads))
    flat_out = jnp.transpose(attn_out, (1, 2, 0, 3)).reshape(tok_count * 2, HEADS * HD)
    velocity = jnp.dot(flat_out.astype(jnp.float32), vel_weight.astype(jnp.float32), preferred_element_type=jnp.float32)
    return (rows_idx, velocity.reshape(WIN_ROWS, WIN_COLS, 2 * LAT))

def reference(img_query, img_key, img_value, text_kv, vel_weight, window_px):
    starts = (window_px // 16).astype(jnp.int32)

    def add_window(canvas, start):
        rows_idx, velocity = window_velocity(start, img_query, img_key, img_value, text_kv, vel_weight)
        return (canvas.at[rows_idx].add(velocity), None)
    canvas, unused = lax.scan(add_window, jnp.zeros((ROWS, WIN_COLS, 2 * LAT), jnp.float32), starts)
    all_rows = jnp.arange(ROWS, dtype=jnp.int32)
    counts = lax.optimization_barrier(jnp.sum((jnp.mod(all_rows[:, None] - starts[None, :], ROWS) < WIN_ROWS).astype(jnp.int32), axis=1))
    canvas_vel = canvas / counts.astype(jnp.float32)[:, None, None]
    cond_vel = canvas_vel[:, :, :LAT]
    delta_vel = cond_vel - canvas_vel[:, :, LAT:]
    sum_dd = jnp.sum(delta_vel * delta_vel)
    sum_dc = jnp.sum(delta_vel * cond_vel)
    sum_cc = jnp.sum(cond_vel * cond_vel)
    clip_limit = clip_rms * math.sqrt(ROWS * WIN_COLS * LAT)
    clip_factor = jnp.minimum(1.0, clip_limit / jnp.sqrt(sum_dd + tiny))
    along_cond = sum_dc / (sum_cc + tiny)
    return cond_vel + (guide_scale - 1.0) * clip_factor * (delta_vel - along_cond * cond_vel)
```

```python
import math

import jax
import jax.numpy as jnp
from jax import lax
from jax.experimental import pallas as pl
from jax.experimental.pallas import tpu as pltpu
from jax.sharding import PartitionSpec as P

HD = 128
HEADS = 16
LAT = 64
TXT = 512
ROWS = 128
WIN_COLS = 64
WINDOWS = 32
SEQ = 16
OWN = 16
TOK = SEQ * OWN

clip_rms = 0.3
guide_scale = 5.0
tiny = 1e-06

SC = math.log2(math.e) / math.sqrt(HD)
LOW = -1e30
FLOOR = -1e29
MESH = pl.DeviceIdType.MESH
f32 = jnp.float32
bf16 = jnp.bfloat16


def mod(value, n):
    return lax.rem(value, jnp.int32(n))


def div(value, n):
    return lax.div(value, jnp.int32(n))


def pick(index, options):
    out = jnp.int32(options[0])
    for n, option in enumerate(options[1:], 1):
        out = jnp.where(index == n, jnp.int32(option), out)
    return out


class Place:
    def __init__(self):
        self.w = w = lax.axis_index("win")
        self.s = s = lax.axis_index("seq")
        self.x, self.y = div(w, 8), mod(w, 8)
        self.p, self.a = div(self.y, 2), mod(self.y, 2)
        self.z, self.c = div(s, 2), mod(s, 2)
        self.base = 8 * self.x + 2 * self.p
        self.block = self.base + self.c
        self.home = 4 * self.x + self.p
        self.head = 2 * self.z + self.a
        self.own_copy = self.c == self.a
        self.me = 2 * self.home + self.c

    def dest(self, d):
        zd, ad = mod(self.z + div(d, 2), SEQ // 2), mod(self.a + mod(d, 2), 2)
        return {"win": self.base + ad, "seq": 2 * zd + self.a}, 2 * zd + ad

    def source(self, d):
        seq = mod(self.s + d, SEQ)
        return {"win": self.base + self.c, "seq": seq}, seq

    def peer(self, g):
        n = mod(self.me + g, 32)
        pair, core = div(n, 2), mod(n, 2)
        return {"win": 8 * div(pair, 4) + 2 * mod(pair, 4) + self.a, "seq": 2 * self.z + core}

    def ring_of(self, j):
        turn = pick(j, (0, 3, 1, 0, 0, 2, 3, 1, 2))
        pp = mod(self.p + turn, 4)
        side = jnp.where(j == 3, 1, jnp.where(j == 4, 3, jnp.where(pp < self.p, 1, 3)))
        far = (j == 3) | (j == 4) | (j >= 6)
        xx = jnp.where(far, mod(self.x + side, 4), self.x)
        place = pp - self.p + 4
        place = jnp.where(far, jnp.where(side == 1, place + 4, place - 4), place)
        return pp, 4 * xx + pp, place

    def send_all(self, copy, keep):
        @pl.when(self.own_copy)
        def _():
            keep().start()

        @pl.when(jnp.logical_not(self.own_copy))
        def _():
            copy(jnp.int32(0)).start()

        @pl.loop(1, SEQ)
        def _(d):
            copy(d).start()


def remote(src, dst, send, recv, to):
    return pltpu.make_async_remote_copy(
        src_ref=src, dst_ref=dst, send_sem=send, recv_sem=recv, device_id=to, device_id_type=MESH
    )


def await_bytes(ref, sem):
    pltpu.make_async_copy(ref, ref, sem).wait()


def hello(to):
    pl.semaphore_signal(pltpu.get_barrier_semaphore(), inc=1, device_id=to, device_id_type=MESH)


def greet_heads(at):
    @pl.loop(1, SEQ)
    def _(d):
        hello(at.dest(d)[0])
        hello(at.source(d)[0])

    @pl.when(jnp.logical_not(at.own_copy))
    def _():
        hello(at.dest(jnp.int32(0))[0])
        hello(at.source(jnp.int32(0))[0])


def collect(
    q_in, k_in, v_in, text_in, wt_in, kv, q_buf, text, wt,
    raw, stage, l_in, s_own, r_own, s_blk, s_sib, r_blk, r_sib, s_text, r_text,
):
    at = Place()
    w, s, x, y, p, a, z, c = at.w, at.s, at.x, at.y, at.p, at.a, at.z, at.c
    home, head, own_copy = at.home, at.head, at.own_copy
    loads = [pltpu.make_async_copy(ref, raw.at[n], l_in.at[n]) for n, ref in enumerate((k_in, v_in, q_in))]
    for load in loads:
        load.start()

    greet_heads(at)
    sibling = {"win": w, "seq": 2 * z + 1 - c}
    up = {"win": 8 * x + 2 * mod(p + 1, 4) + a, "seq": s}
    down = {"win": 8 * x + 2 * mod(p + 3, 4) + a, "seq": s}
    hello(sibling)
    hello(up)
    hello(down)
    hello({"win": 8 * mod(x + 1, 4) + y, "seq": s})
    hello({"win": 8 * mod(x + 3, 4) + y, "seq": s})

    for n, load in enumerate(loads):
        load.wait()
        flat = raw[n].reshape(OWN, HEADS * HD)
        for h in range(HEADS):
            stage[n, h] = flat[:, h * HD : (h + 1) * HD]

    pl.semaphore_wait(pltpu.get_barrier_semaphore(), jnp.where(own_copy, 2 * SEQ + 3, 2 * SEQ + 5))

    rows = pl.ds(pl.multiple_of(OWN * s, OWN), OWN)
    for n in range(3):
        dst = q_buf.at[rows, :] if n == 2 else kv.at[home, a, n, rows, :]

        def give(d, n=n, dst=dst):
            to, h = at.dest(d)
            return remote(stage.at[n, h], dst, s_own.at[0], r_own.at[n], to)

        def keep(n=n, dst=dst):
            return pltpu.make_async_copy(stage.at[n, head], dst, r_own.at[n])

        at.send_all(give, keep)


    def text_sends():
        return (
            remote(text_in, text, s_text.at[0], r_text.at[0], sibling),
            remote(wt_in, wt, s_text.at[1], r_text.at[1], sibling),
        )

    @pl.when(own_copy)
    def _():
        pltpu.make_async_copy(text_in, text, r_text.at[0]).start()
        pltpu.make_async_copy(wt_in, wt, r_text.at[1]).start()
        for copy in text_sends():
            copy.start()

    def blk(pair, core, n):
        return kv.at[pair, core, n]

    def send_block(n, pair, step, to, sem):
        remote(blk(pair, c, n), blk(pair, c, n), s_blk.at[sem, n], r_blk.at[step, n], to).start()

    def send_x(n, pair, step, side):
        send_block(n, pair, step, {"win": 8 * mod(x + side, 4) + y, "seq": s}, step)

    def send_sib(n, pair, step):
        remote(blk(pair, c, n), blk(pair, c, n), s_sib.at[step, n], r_sib.at[step, n], sibling).start()

    def arrived(n, pair, step):
        await_bytes(blk(pair, c, n), r_blk.at[step, n])

    def hand_on(n, step, x_step):
        pp, pair, _ = at.ring_of(jnp.int32(step))
        arrived(n, pair, step)
        if step == 1 and n == 0:
            send_block(n, pair, 5, up, 5)
        if step == 2 and n == 1:
            send_block(n, pair, 5, down, 5)
        send_x(n, pair, x_step, jnp.where(pp < p, 3, 1))
        send_sib(n, pair, step)

    await_bytes(blk(home, c, 0), r_own.at[0])
    send_block(0, home, 1, up, 1)
    send_x(0, home, 4, 1)
    send_x(0, home, 3, 3)
    send_sib(0, home, 0)
    await_bytes(blk(home, c, 1), r_own.at[1])
    send_block(1, home, 2, down, 2)
    send_block(1, home, 1, up, 1)
    send_block(0, home, 2, down, 2)
    send_x(1, home, 4, 1)
    send_x(1, home, 3, 3)
    send_sib(1, home, 0)
    await_bytes(q_buf, r_own.at[2])

    @pl.loop(0, 9)
    def _(j):
        _, pair, _ = at.ring_of(j)

        @pl.when(j == 1)
        def _():
            hand_on(0, 1, 6)
            hand_on(1, 2, 7)
            hand_on(1, 1, 6)
            hand_on(0, 2, 7)

        @pl.when(j == 5)
        def _():
            hand_on(0, 5, 8)
            hand_on(1, 5, 8)

        @pl.when((j == 3) | (j == 4) | (j >= 6))
        def _():
            for n in range(2):
                arrived(n, pair, j)
                send_sib(n, pair, j)

    @pl.loop(0, 9)
    def _(j):
        _, pair, _ = at.ring_of(j)
        for n in range(2):
            await_bytes(blk(pair, 1 - c, n), r_sib.at[j, n])

    for n in range(2):
        await_bytes((text, wt)[n], r_text.at[n])

    @pl.when(own_copy)
    def _():
        for copy in text_sends():
            copy.wait_send()
        await_bytes(stage.at[:, pl.ds(0, SEQ - 1)], s_own.at[0])

    @pl.when(jnp.logical_not(own_copy))
    def _():
        await_bytes(stage, s_own.at[0])

    @pl.loop(0, 9)
    def _(j):
        for n in range(2):
            await_bytes(blk(home, c, n), s_sib.at[j, n])

        @pl.when(j > 0)
        def _():
            for n in range(2):
                await_bytes(blk(home, c, n), s_blk.at[j, n])


def mix(
    q_buf, kv, text, wt, px, vel, qt_buf, part, top, low, ptext, coef, attn, starts,
):
    at = Place()
    block, c = at.block, at.c

    def scan_start(n, found):
        start = div(px[n], 16)
        slot = div(start, 4)
        off = start - 4 * slot
        return tuple(
            old + jnp.where(slot == mod(block + 24 + i, 32), off, 0) for i, old in enumerate(found)
        )

    offsets = lax.fori_loop(0, WINDOWS, scan_start, (jnp.int32(0),) * 9)
    for i in range(9):
        starts[i] = offsets[i]

    qt_buf[...] = q_buf[...].T

    def segment(scores, values_t):
        peak = jnp.maximum(jnp.max(scores, axis=0, keepdims=True), FLOOR)
        weights = jnp.exp2((scores - peak) * SC)
        total = jnp.sum(weights, axis=0, keepdims=True)
        return peak, total, jnp.dot(values_t, weights.astype(bf16), preferred_element_type=f32)

    def attend(pair, core, place):
        b = 2 * place + core - c
        scores = jnp.dot(kv[pair, core, 0], qt_buf[...], preferred_element_type=f32)
        values_t = kv[pair, core, 1].T
        key_row = mod(div(lax.broadcasted_iota(jnp.int32, (TOK, 1), 0), 4), 4)

        def keep(kind, masked):
            peak, total, mix = segment(masked, values_t)
            row = b + 1
            top[kind, pl.ds(row, 1), :] = peak
            low[kind, pl.ds(row, 1), :] = total
            part[kind, row] = mix

        keep(0, scores)
        begins = b <= 8
        bound = starts[jnp.clip(jnp.where(begins, b, b - 8), 0, 8)]
        first = jnp.where(begins, bound, 0)
        last = jnp.where(begins, 4, bound)
        inside = (key_row >= first) & (key_row < last)
        keep(1, scores + jnp.where(inside, 0.0, LOW))

        @pl.when(b == 8)
        def _():
            peak, total, mix = segment(scores + jnp.where(key_row < starts[0], 0.0, LOW), values_t)
            top[2, 0:1, :] = peak
            low[2, 0:1, :] = total
            part[2, 0] = mix

    @pl.loop(0, 2)
    def _(branch):
        scores = jnp.dot(text[branch, 0], qt_buf[...], preferred_element_type=f32)
        peak, total, mix = segment(scores, text[branch, 1].T)
        top[2, pl.ds(8 + branch, 1), :] = peak
        low[2, pl.ds(8 + branch, 1), :] = total
        ptext[branch] = mix

    @pl.loop(0, 9)
    def _(j):
        pair = mod(at.home + 12 + j, 16)
        attend(pair, 0, j)
        attend(pair, 1, j)

    query_row = mod(div(lax.broadcasted_iota(jnp.int32, (1, TOK), 1), 4), 4)
    holds_first = (query_row < starts[0]).astype(f32)
    holds_last = (query_row >= starts[8]).astype(f32)
    share = 1.0 / (7.0 + holds_first + holds_last)
    which = lax.broadcasted_iota(jnp.int32, (9, TOK), 0)
    member = jnp.where(which == 0, holds_first * share, jnp.where(which == 8, holds_last * share, share))

    head_top, head_low = top[1, 1:10, :], low[1, 1:10, :]
    tail_top = jnp.concatenate([top[2, 0:1, :], top[1, 10:18, :]], axis=0)
    tail_low = jnp.concatenate([low[2, 0:1, :], low[1, 10:18, :]], axis=0)
    peak = jnp.maximum(head_top, tail_top)
    for d in range(1, 8):
        peak = jnp.maximum(peak, top[0, 1 + d : 10 + d, :])
    e_head = jnp.exp2((head_top - peak) * SC)
    e_tail = jnp.exp2((tail_top - peak) * SC)
    total = e_head * head_low + e_tail * tail_low
    e_full = []
    for d in range(1, 8):
        e_full.append(jnp.exp2((top[0, 1 + d : 10 + d, :] - peak) * SC))
        total = total + e_full[-1] * low[0, 1 + d : 10 + d, :]
    coef[...] = jnp.zeros_like(coef)
    for branch in range(2):
        text_top, text_low = top[2, 8 + branch : 9 + branch, :], low[2, 8 + branch : 9 + branch, :]
        both = jnp.maximum(peak, text_top)
        e_img = jnp.exp2((peak - both) * SC)
        e_text = jnp.exp2((text_top - both) * SC)
        scale = member / (e_img * total + e_text * text_low)
        gain = e_img * scale
        for d in range(1, 8):
            coef[branch, 0, 1 + d : 10 + d, :] += gain * e_full[d - 1]
        coef[branch, 1, 1:10, :] = gain * e_head
        coef[branch, 2, 0:9, :] = gain * e_tail
        coef[branch, 2, 9:10, :] = jnp.sum(e_text * scale, axis=0, keepdims=True)

    @pl.loop(0, 8)
    def _(chunk):
        feats = pl.ds(pl.multiple_of(chunk * 16, 16), 16)
        sums = [jnp.zeros((16, TOK), f32), jnp.zeros((16, TOK), f32)]

        def add(value, kind, row):
            for branch in range(2):
                sums[branch] = sums[branch] + value * coef[branch, kind, row : row + 1, :]

        for b in range(1, 16):
            add(part[0, b + 1, feats, :], 0, b + 1)
        for b in range(0, 9):
            add(part[1, b + 1, feats, :], 1, b + 1)
        add(part[2, 0, feats, :], 2, 0)
        for b in range(9, 17):
            add(part[1, b + 1, feats, :], 2, b - 8)
        for branch in range(2):
            mixed = sums[branch] + ptext[branch, feats, :] * coef[branch, 2, 9:10, :]
            main = mixed.astype(bf16)
            attn[pl.ds(pl.multiple_of(branch * HD + chunk * 16, 16), 16), :] = main
            attn[pl.ds(pl.multiple_of((2 + branch) * HD + chunk * 16, 16), 16), :] = (
                mixed - main.astype(f32)
            ).astype(bf16)

    proj = wt[...]
    proj = jnp.concatenate(
        [
            jnp.concatenate([proj, jnp.zeros_like(proj)], axis=1),
            jnp.concatenate([proj, -proj], axis=1),
        ],
        axis=0,
    )
    proj = jnp.concatenate([proj, proj], axis=1)
    vel[...] = jnp.dot(proj, attn[...], preferred_element_type=f32).T.astype(bf16)


def finish(vel, out_ref, rs, st, st2, ar1, ar2, s_sum, r_sum):
    at = Place()
    s, head, me, own_copy = at.s, at.head, at.me, at.own_copy
    rows = pl.ds(pl.multiple_of(OWN * s, OWN), OWN)
    greet_heads(at)

    @pl.loop(1, 32)
    def _(g):
        hello(at.peer(g))

    pl.semaphore_wait(pltpu.get_barrier_semaphore(), jnp.where(own_copy, 2 * SEQ + 29, 2 * SEQ + 31))

    def rs_copy(d):
        to, seq = at.source(d)
        there = pl.ds(pl.multiple_of(OWN * seq, OWN), OWN)
        return remote(vel.at[there, :], rs.at[head], s_sum.at[0], r_sum.at[0], to)

    at.send_all(rs_copy, lambda: pltpu.make_async_copy(vel.at[rows, :], rs.at[head], r_sum.at[0]))
    await_bytes(rs, r_sum.at[0])

    mine = jnp.sum(rs[...].astype(f32), axis=0)
    turned = pltpu.roll(mine, LAT, 1)
    st[...] = jnp.concatenate(
        [jnp.sum(mine * mine, axis=0, keepdims=True), jnp.sum(mine * turned, axis=0, keepdims=True)], axis=0
    )

    def a1_copy(d):
        return remote(st, ar1.at[s], s_sum.at[1], r_sum.at[1], at.dest(d)[0])

    at.send_all(a1_copy, lambda: pltpu.make_async_copy(st, ar1.at[s], r_sum.at[1]))
    await_bytes(ar1, r_sum.at[1])
    st2[...] = jnp.sum(ar1[...], axis=0)

    @pl.loop(1, 32)
    def _(g):
        remote(st2, ar2.at[me], s_sum.at[2], r_sum.at[2], at.peer(g)).start()

    pltpu.make_async_copy(st2, ar2.at[me], r_sum.at[2]).start()
    await_bytes(ar2, r_sum.at[2])
    sums = jnp.sum(ar2[...], axis=0)
    is_cond = lax.broadcasted_iota(jnp.int32, (1, 2 * LAT), 1) < LAT
    s_cc = jnp.sum(jnp.where(is_cond, sums[0:1, :], 0.0), axis=1, keepdims=True)
    s_dd = jnp.sum(jnp.where(is_cond, 0.0, sums[0:1, :]), axis=1, keepdims=True)
    s_dc = jnp.sum(jnp.where(is_cond, sums[1:2, :], 0.0), axis=1, keepdims=True)
    clip_limit = clip_rms * math.sqrt(ROWS * WIN_COLS * LAT)
    clip_factor = jnp.minimum(1.0, clip_limit / jnp.sqrt(s_dd + tiny))
    along = s_dc / (s_cc + tiny)
    guided = mine + (guide_scale - 1.0) * clip_factor * (turned - along * mine)
    out_ref[...] = guided[:, :LAT]

    @pl.when(own_copy)
    def _():
        await_bytes(rs.at[pl.ds(0, SEQ - 1)], s_sum.at[0])
        await_bytes(ar1.at[pl.ds(0, SEQ - 1)], s_sum.at[1])

    @pl.when(jnp.logical_not(own_copy))
    def _():
        await_bytes(rs, s_sum.at[0])
        await_bytes(ar1, s_sum.at[1])

    await_bytes(ar2.at[pl.ds(0, 31)], s_sum.at[2])


def local(img_query, img_key, img_value, text_kv, vel_weight, window_px):
    dma = pltpu.SemaphoreType.DMA
    vmem = pl.BlockSpec(memory_space=pltpu.VMEM)
    kv, queries, text, wt = pl.pallas_call(
        collect,
        out_shape=[
            jax.ShapeDtypeStruct((16, 2, 2, TOK, HD), bf16),
            jax.ShapeDtypeStruct((TOK, HD), bf16),
            jax.ShapeDtypeStruct((2, 2, TXT, HD), bf16),
            jax.ShapeDtypeStruct((LAT, HD), bf16),
        ],
        in_specs=[pl.BlockSpec(memory_space=pltpu.HBM)] * 5,
        out_specs=[vmem] * 4,
        scratch_shapes=[
            pltpu.VMEM((3, 4, 4, HEADS * HD), bf16),
            pltpu.VMEM((3, HEADS, OWN, HD), bf16),
            dma((3,)),
            dma((1,)),
            dma((3,)),
            dma((9, 2)),
            dma((9, 2)),
            dma((9, 2)),
            dma((9, 2)),
            dma((2,)),
            dma((2,)),
        ],
        compiler_params=pltpu.CompilerParams(collective_id=0, has_side_effects=True, vmem_limit_bytes=16 * 2**20),
    )(img_query, img_key, img_value, text_kv, vel_weight.T)
    vel = pl.pallas_call(
        mix,
        out_shape=jax.ShapeDtypeStruct((TOK, 2 * LAT), bf16),
        in_specs=[vmem] * 4 + [pl.BlockSpec(memory_space=pltpu.SMEM)],
        out_specs=vmem,
        scratch_shapes=[
            pltpu.VMEM((HD, TOK), bf16),
            pltpu.VMEM((3, 19, HD, TOK), f32),
            pltpu.VMEM((3, 24, TOK), f32),
            pltpu.VMEM((3, 24, TOK), f32),
            pltpu.VMEM((2, HD, TOK), f32),
            pltpu.VMEM((2, 3, 24, TOK), f32),
            pltpu.VMEM((4 * HD, TOK), bf16),
            pltpu.SMEM((9,), jnp.int32),
        ],
        compiler_params=pltpu.CompilerParams(vmem_limit_bytes=24 * 2**20),
    )(queries, kv, text, wt, window_px)
    out = pl.pallas_call(
        finish,
        out_shape=jax.ShapeDtypeStruct((OWN, LAT), f32),
        in_specs=[vmem],
        out_specs=vmem,
        scratch_shapes=[
            pltpu.VMEM((HEADS, OWN, 2 * LAT), bf16),
            pltpu.VMEM((2, 2 * LAT), f32),
            pltpu.VMEM((2, 2 * LAT), f32),
            pltpu.VMEM((SEQ, 2, 2 * LAT), f32),
            pltpu.VMEM((32, 2, 2 * LAT), f32),
            dma((3,)),
            dma((3,)),
        ],
        compiler_params=pltpu.CompilerParams(collective_id=1, has_side_effects=True),
    )(vel)
    return out.reshape(4, 4, LAT)


def solution(mesh):
    in_specs = (
        P("win", "seq", None),
        P("win", "seq", None),
        P("win", "seq", None),
        P(None, None, None, "seq"),
        P("seq", None),
        P(),
    )
    out_specs = P("win", "seq", None)
    return jax.shard_map(local, mesh=mesh, in_specs=in_specs, out_specs=out_specs, check_vma=False)
```

```python
import math

import jax
import jax.numpy as jnp
from jax import lax
from jax.experimental import pallas as pl
from jax.experimental.pallas import tpu as pltpu
from jax.sharding import PartitionSpec as P

HD = 128
HEADS = 16
LAT = 64
TXT = 512
ROWS = 128
WIN_COLS = 64
WINDOWS = 32
SEQ = 16
OWN = 16
TOK = SEQ * OWN

clip_rms = 0.3
guide_scale = 5.0
tiny = 1e-06

SC = math.log2(math.e) / math.sqrt(HD)
LOW = -1e30
FLOOR = -1e29
MESH = pl.DeviceIdType.MESH
f32 = jnp.float32
bf16 = jnp.bfloat16


def mod(value, n):
    return lax.rem(value, jnp.int32(n))


def div(value, n):
    return lax.div(value, jnp.int32(n))


def pick(index, options):
    out = jnp.int32(options[0])
    for n, option in enumerate(options[1:], 1):
        out = jnp.where(index == n, jnp.int32(option), out)
    return out


def kernel(
    q_in, k_in, v_in, text_in, wt_in, px, out_ref,
    raw, stage, kvd, kvs, q_buf, qt_buf, text, wt, part, top, low, ptext, coef, attn, vel, rs, st, st2, ar1, ar2, starts,
    l_in, s_own, r_own, s_blk, s_sib, r_blk, r_sib, s_text, r_text, s_sum, r_sum,
):
    w = lax.axis_index("win")
    s = lax.axis_index("seq")
    x, y = div(w, 8), mod(w, 8)
    p, a = div(y, 2), mod(y, 2)
    z, c = div(s, 2), mod(s, 2)
    base = 8 * x + 2 * p
    block = base + c
    home = 4 * x + p
    head = 2 * z + a
    own_copy = c == a
    zero = jnp.int32(0)

    def dest(d):
        zd, ad = mod(z + div(d, 2), SEQ // 2), mod(a + mod(d, 2), 2)
        return {"win": base + ad, "seq": 2 * zd + a}, 2 * zd + ad

    def source(d):
        return {"win": base + c, "seq": mod(s + d, SEQ)}, mod(s + d, SEQ)

    def along_seq(d):
        return {"win": w, "seq": mod(s + d, SEQ)}

    def along_win(g):
        return {"win": mod(w + g, 32), "seq": s}

    def remote(src, dst, send, recv, to):
        return pltpu.make_async_remote_copy(
            src_ref=src, dst_ref=dst, send_sem=send, recv_sem=recv, device_id=to, device_id_type=MESH
        )

    def await_bytes(ref, sem):
        pltpu.make_async_copy(ref, ref, sem).wait()

    def send_all(copy, keep):
        @pl.when(own_copy)
        def _():
            keep().start()

        @pl.when(jnp.logical_not(own_copy))
        def _():
            copy(zero).start()

        @pl.loop(1, SEQ)
        def _(d):
            copy(d).start()

    loads = [pltpu.make_async_copy(ref, raw.at[n], l_in.at[n]) for n, ref in enumerate((k_in, v_in, q_in))]
    for load in loads:
        load.start()

    barrier = pltpu.get_barrier_semaphore()

    def hello(to):
        pl.semaphore_signal(barrier, inc=1, device_id=to, device_id_type=MESH)

    @pl.loop(1, SEQ)
    def _(d):
        hello(dest(d)[0])
        hello(source(d)[0])
        hello(along_seq(d))

    @pl.when(jnp.logical_not(own_copy))
    def _():
        hello(dest(zero)[0])
        hello(source(zero)[0])

    @pl.loop(1, 32)
    def _(g):
        hello(along_win(g))

    rows = pl.ds(pl.multiple_of(OWN * s, OWN), OWN)
    for n, load in enumerate(loads):
        load.wait()
        flat = raw[n].reshape(OWN, HEADS * HD)
        for h in range(HEADS):
            stage[n, h] = flat[:, h * HD : (h + 1) * HD]
        if n == 0:
            pl.semaphore_wait(barrier, jnp.where(own_copy, 3 * SEQ + 28, 3 * SEQ + 30))
        dst = q_buf.at[rows, :] if n == 2 else kvd.at[0, n, rows, :]

        def give(d, n=n, dst=dst):
            to, h = dest(d)
            return remote(stage.at[n, h], dst, s_own.at[0], r_own.at[n], to)

        def keep(n=n, dst=dst):
            return pltpu.make_async_copy(stage.at[n, head], dst, r_own.at[n])

        send_all(give, keep)

    sibling = {"win": w, "seq": 2 * z + 1 - c}

    def text_sends():
        return (
            remote(text_in, text, s_text.at[0], r_text.at[0], sibling),
            remote(wt_in, wt, s_text.at[1], r_text.at[1], sibling),
        )

    @pl.when(own_copy)
    def _():
        pltpu.make_async_copy(text_in, text, r_text.at[0]).start()
        pltpu.make_async_copy(wt_in, wt, r_text.at[1]).start()
        for copy in text_sends():
            copy.start()

    def place_of(j):
        turn = pick(j, (0, 3, 1, 0, 0, 2, 3, 1, 2))
        pp = mod(p + turn, 4)
        side = jnp.where(j == 3, 1, jnp.where(j == 4, 3, jnp.where(pp < p, 1, 3)))
        far = (j == 3) | (j == 4) | (j >= 6)
        place = pp - p + 4
        place = jnp.where(far, jnp.where(side == 1, place + 4, place - 4), place)
        return place

    up = {"win": 8 * x + 2 * mod(p + 1, 4) + a, "seq": s}
    down = {"win": 8 * x + 2 * mod(p + 3, 4) + a, "seq": s}

    def send_block(n, have, step, to):
        remote(kvd.at[have, n], kvd.at[step, n], s_blk.at[step, n], r_blk.at[step, n], to).start()

    def send_x(n, have, step, side):
        send_block(n, have, step, {"win": 8 * mod(x + side, 4) + y, "seq": s})

    def send_sib(n, step):
        remote(kvd.at[step, n], kvs.at[step, n], s_sib.at[step, n], r_sib.at[step, n], sibling).start()

    def hand_on(n, step, turn, x_step):
        await_bytes(kvd.at[step, n], r_blk.at[step, n])
        if step == 1 and n == 0:
            send_block(n, step, 5, up)
        if step == 2 and n == 1:
            send_block(n, step, 5, down)
        send_x(n, step, x_step, jnp.where(mod(p + turn, 4) < p, 3, 1))
        send_sib(n, step)

    await_bytes(kvd.at[0, 0], r_own.at[0])
    send_block(0, 0, 1, up)
    send_x(0, 0, 4, 1)
    send_x(0, 0, 3, 3)
    send_sib(0, 0)
    await_bytes(kvd.at[0, 1], r_own.at[1])
    send_block(1, 0, 2, down)
    send_block(1, 0, 1, up)
    send_block(0, 0, 2, down)
    send_x(1, 0, 4, 1)
    send_x(1, 0, 3, 3)
    send_sib(1, 0)
    def scan_start(n, found):
        start = div(px[n], 16)
        slot = div(start, 4)
        off = start - 4 * slot
        return tuple(
            old + jnp.where(slot == mod(block + 24 + i, 32), off, 0) for i, old in enumerate(found)
        )

    offsets = lax.fori_loop(0, WINDOWS, scan_start, (zero,) * 9)
    for i in range(9):
        starts[i] = offsets[i]

    await_bytes(q_buf, r_own.at[2])

    qt_buf[...] = q_buf[...].T

    def segment(scores, values_t):
        peak = jnp.maximum(jnp.max(scores, axis=0, keepdims=True), FLOOR)
        weights = jnp.exp2((scores - peak) * SC)
        total = jnp.sum(weights, axis=0, keepdims=True)
        return peak, total, jnp.dot(values_t, weights.astype(bf16), preferred_element_type=f32)

    def attend(held, j, core, place):
        b = 2 * place + core - c
        scores = jnp.dot(held[j, 0], qt_buf[...], preferred_element_type=f32)
        values_t = held[j, 1].T
        key_row = mod(div(lax.broadcasted_iota(jnp.int32, (TOK, 1), 0), 4), 4)

        def keep(kind, masked):
            peak, total, mix = segment(masked, values_t)
            row = b + 1
            top[kind, pl.ds(row, 1), :] = peak
            low[kind, pl.ds(row, 1), :] = total
            part[kind, row] = mix

        keep(0, scores)
        begins = b <= 8
        bound = starts[jnp.clip(jnp.where(begins, b, b - 8), 0, 8)]
        first = jnp.where(begins, bound, 0)
        last = jnp.where(begins, 4, bound)
        inside = (key_row >= first) & (key_row < last)
        keep(1, scores + jnp.where(inside, 0.0, LOW))

        @pl.when(b == 8)
        def _():
            peak, total, mix = segment(scores + jnp.where(key_row < starts[0], 0.0, LOW), values_t)
            top[2, 0:1, :] = peak
            low[2, 0:1, :] = total
            part[2, 0] = mix

    def text_part():
        for n in range(2):
            pltpu.make_async_copy((text_in, wt_in)[n], (text, wt)[n], r_text.at[n]).wait()

        @pl.loop(0, 2)
        def _(branch):
            scores = jnp.dot(text[branch, 0], qt_buf[...], preferred_element_type=f32)
            peak, total, mix = segment(scores, text[branch, 1].T)
            top[2, pl.ds(8 + branch, 1), :] = peak
            low[2, pl.ds(8 + branch, 1), :] = total
            ptext[branch] = mix

    @pl.loop(0, 9)
    def _(j):
        place = place_of(j)

        def pass_on(step):
            for n in range(2):
                await_bytes(kvd.at[step, n], r_blk.at[step, n])
                send_sib(n, step)

        @pl.when(j == 1)
        def _():
            hand_on(0, 1, 3, 6)
            hand_on(1, 2, 1, 7)
            hand_on(1, 1, 3, 6)
            hand_on(0, 2, 1, 7)
            pass_on(3)
            pass_on(4)

        @pl.when(j == 3)
        def _():
            hand_on(0, 5, 2, 8)
            hand_on(1, 5, 2, 8)

        @pl.when(j == 5)
        def _():
            pass_on(6)
            pass_on(7)

        @pl.when(j == 8)
        def _():
            pass_on(8)

        attend(kvd, j, c, place)

        @pl.when(j == 0)
        def _():
            text_part()

        for n in range(2):
            await_bytes(kvs.at[j, n], r_sib.at[j, n])
        attend(kvs, j, 1 - c, place)

    query_row = mod(div(lax.broadcasted_iota(jnp.int32, (1, TOK), 1), 4), 4)
    holds_first = (query_row < starts[0]).astype(f32)
    holds_last = (query_row >= starts[8]).astype(f32)
    share = 1.0 / (7.0 + holds_first + holds_last)
    which = lax.broadcasted_iota(jnp.int32, (9, TOK), 0)
    member = jnp.where(which == 0, holds_first * share, jnp.where(which == 8, holds_last * share, share))

    head_top, head_low = top[1, 1:10, :], low[1, 1:10, :]
    tail_top = jnp.concatenate([top[2, 0:1, :], top[1, 10:18, :]], axis=0)
    tail_low = jnp.concatenate([low[2, 0:1, :], low[1, 10:18, :]], axis=0)
    peak = jnp.maximum(head_top, tail_top)
    for d in range(1, 8):
        peak = jnp.maximum(peak, top[0, 1 + d : 10 + d, :])
    e_head = jnp.exp2((head_top - peak) * SC)
    e_tail = jnp.exp2((tail_top - peak) * SC)
    total = e_head * head_low + e_tail * tail_low
    e_full = []
    for d in range(1, 8):
        e_full.append(jnp.exp2((top[0, 1 + d : 10 + d, :] - peak) * SC))
        total = total + e_full[-1] * low[0, 1 + d : 10 + d, :]
    coef[...] = jnp.zeros_like(coef)
    for branch in range(2):
        text_top, text_low = top[2, 8 + branch : 9 + branch, :], low[2, 8 + branch : 9 + branch, :]
        both = jnp.maximum(peak, text_top)
        e_img = jnp.exp2((peak - both) * SC)
        e_text = jnp.exp2((text_top - both) * SC)
        scale = member / (e_img * total + e_text * text_low)
        gain = e_img * scale
        for d in range(1, 8):
            coef[branch, 0, 1 + d : 10 + d, :] += gain * e_full[d - 1]
        coef[branch, 1, 1:10, :] = gain * e_head
        coef[branch, 2, 0:9, :] = gain * e_tail
        coef[branch, 2, 9:10, :] = jnp.sum(e_text * scale, axis=0, keepdims=True)

    @pl.loop(0, 8)
    def _(chunk):
        feats = pl.ds(pl.multiple_of(chunk * 16, 16), 16)
        sums = [jnp.zeros((16, TOK), f32), jnp.zeros((16, TOK), f32)]

        def add(value, kind, row):
            for branch in range(2):
                sums[branch] = sums[branch] + value * coef[branch, kind, row : row + 1, :]

        for b in range(1, 16):
            add(part[0, b + 1, feats, :], 0, b + 1)
        for b in range(0, 9):
            add(part[1, b + 1, feats, :], 1, b + 1)
        add(part[2, 0, feats, :], 2, 0)
        for b in range(9, 17):
            add(part[1, b + 1, feats, :], 2, b - 8)
        for branch in range(2):
            mixed = sums[branch] + ptext[branch, feats, :] * coef[branch, 2, 9:10, :]
            main = mixed.astype(bf16)
            attn[pl.ds(pl.multiple_of(branch * HD + chunk * 16, 16), 16), :] = main
            attn[pl.ds(pl.multiple_of((2 + branch) * HD + chunk * 16, 16), 16), :] = (
                mixed - main.astype(f32)
            ).astype(bf16)

    proj = wt[...]
    proj = jnp.concatenate(
        [
            jnp.concatenate([proj, jnp.zeros_like(proj)], axis=1),
            jnp.concatenate([proj, -proj], axis=1),
        ],
        axis=0,
    )
    proj = jnp.concatenate([proj, proj], axis=1)
    vel[...] = jnp.dot(proj, attn[...], preferred_element_type=f32).T.astype(bf16)

    def rs_copy(d):
        to, seq = source(d)
        there = pl.ds(pl.multiple_of(OWN * seq, OWN), OWN)
        return remote(vel.at[there, :], rs.at[head], s_sum.at[0], r_sum.at[0], to)

    send_all(rs_copy, lambda: pltpu.make_async_copy(vel.at[rows, :], rs.at[head], r_sum.at[0]))
    await_bytes(rs, r_sum.at[0])

    mine = jnp.sum(rs[...].astype(f32), axis=0)
    turned = pltpu.roll(mine, LAT, 1)
    st[...] = jnp.concatenate(
        [jnp.sum(mine * mine, axis=0, keepdims=True), jnp.sum(mine * turned, axis=0, keepdims=True)], axis=0
    )

    @pl.loop(1, SEQ)
    def _(d):
        remote(st, ar1.at[s], s_sum.at[1], r_sum.at[1], along_seq(d)).start()

    pltpu.make_async_copy(st, ar1.at[s], r_sum.at[1]).start()
    await_bytes(ar1, r_sum.at[1])
    st2[...] = jnp.sum(ar1[...], axis=0)

    @pl.loop(1, 32)
    def _(g):
        remote(st2, ar2.at[w], s_sum.at[2], r_sum.at[2], along_win(g)).start()

    pltpu.make_async_copy(st2, ar2.at[w], r_sum.at[2]).start()
    await_bytes(ar2, r_sum.at[2])
    sums = jnp.sum(ar2[...], axis=0)
    is_cond = lax.broadcasted_iota(jnp.int32, (1, 2 * LAT), 1) < LAT
    s_cc = jnp.sum(jnp.where(is_cond, sums[0:1, :], 0.0), axis=1, keepdims=True)
    s_dd = jnp.sum(jnp.where(is_cond, 0.0, sums[0:1, :]), axis=1, keepdims=True)
    s_dc = jnp.sum(jnp.where(is_cond, sums[1:2, :], 0.0), axis=1, keepdims=True)
    clip_limit = clip_rms * math.sqrt(ROWS * WIN_COLS * LAT)
    clip_factor = jnp.minimum(1.0, clip_limit / jnp.sqrt(s_dd + tiny))
    along = s_dc / (s_cc + tiny)
    guided = mine + (guide_scale - 1.0) * clip_factor * (turned - along * mine)
    out_ref[...] = guided[:, :LAT]

    @pl.when(own_copy)
    def _():
        for copy in text_sends():
            copy.wait_send()
        most = pl.ds(0, SEQ - 1)
        await_bytes(stage.at[:, most], s_own.at[0])
        await_bytes(rs.at[most], s_sum.at[0])

    @pl.when(jnp.logical_not(own_copy))
    def _():
        await_bytes(stage, s_own.at[0])
        await_bytes(rs, s_sum.at[0])

    await_bytes(ar1.at[pl.ds(0, SEQ - 1)], s_sum.at[1])
    await_bytes(ar2.at[pl.ds(0, 31)], s_sum.at[2])
    @pl.loop(0, 9)
    def _(j):
        for n in range(2):
            await_bytes(kvd.at[0, n], s_sib.at[j, n])

        @pl.when(j > 0)
        def _():
            for n in range(2):
                await_bytes(kvd.at[0, n], s_blk.at[j, n])


def local(img_query, img_key, img_value, text_kv, vel_weight, window_px):
    dma = pltpu.SemaphoreType.DMA
    anywhere = pl.BlockSpec(memory_space=pl.ANY)
    out = pl.pallas_call(
        kernel,
        out_shape=jax.ShapeDtypeStruct((OWN, LAT), f32),
        in_specs=[anywhere] * 5 + [pl.BlockSpec(memory_space=pltpu.SMEM)],
        out_specs=pl.BlockSpec(memory_space=pltpu.VMEM),
        scratch_shapes=[
            pltpu.VMEM((3, 4, 4, HEADS * HD), bf16),
            pltpu.VMEM((3, HEADS, OWN, HD), bf16),
            pltpu.VMEM((9, 2, TOK, HD), bf16),
            pltpu.VMEM((9, 2, TOK, HD), bf16),
            pltpu.VMEM((TOK, HD), bf16),
            pltpu.VMEM((HD, TOK), bf16),
            pltpu.VMEM((2, 2, TXT, HD), bf16),
            pltpu.VMEM((LAT, HD), bf16),
            pltpu.VMEM((3, 19, HD, TOK), f32),
            pltpu.VMEM((3, 24, TOK), f32),
            pltpu.VMEM((3, 24, TOK), f32),
            pltpu.VMEM((2, HD, TOK), f32),
            pltpu.VMEM((2, 3, 24, TOK), f32),
            pltpu.VMEM((4 * HD, TOK), bf16),
            pltpu.VMEM((TOK, 2 * LAT), bf16),
            pltpu.VMEM((HEADS, OWN, 2 * LAT), bf16),
            pltpu.VMEM((2, 2 * LAT), f32),
            pltpu.VMEM((2, 2 * LAT), f32),
            pltpu.VMEM((SEQ, 2, 2 * LAT), f32),
            pltpu.VMEM((32, 2, 2 * LAT), f32),
            pltpu.SMEM((9,), jnp.int32),
            dma((3,)),
            dma((1,)),
            dma((3,)),
            dma((9, 2)),
            dma((9, 2)),
            dma((9, 2)),
            dma((9, 2)),
            dma((2,)),
            dma((2,)),
            dma((3,)),
            dma((3,)),
        ],
        compiler_params=pltpu.CompilerParams(
            collective_id=0, has_side_effects=True, vmem_limit_bytes=60 * 2**20
        ),
    )(img_query, img_key, img_value, text_kv, vel_weight.T, window_px)
    return out.reshape(4, 4, LAT)


def solution(mesh):
    in_specs = (
        P("win", "seq", None),
        P("win", "seq", None),
        P("win", "seq", None),
        P(None, None, None, "seq"),
        P("seq", None),
        P(),
    )
    out_specs = P("win", "seq", None)
    return jax.shard_map(local, mesh=mesh, in_specs=in_specs, out_specs=out_specs, check_vma=False)
```

```python
import math

import jax
import jax.numpy as jnp
from jax import lax
from jax.experimental import pallas as pl
from jax.experimental.pallas import tpu as pltpu
from jax.sharding import PartitionSpec as P

HD = 128
HEADS = 16
LAT = 64
TXT = 512
ROWS = 128
WIN_COLS = 64
WINDOWS = 32
SEQ = 16
OWN = 16
TOK = SEQ * OWN

clip_rms = 0.3
guide_scale = 5.0
tiny = 1e-06

SC = math.log2(math.e) / math.sqrt(HD)
LOW = -1e30
FLOOR = -1e29
MESH = pl.DeviceIdType.MESH
f32 = jnp.float32
bf16 = jnp.bfloat16


def mod(value, n):
    return lax.rem(value, jnp.int32(n))


def div(value, n):
    return lax.div(value, jnp.int32(n))


def pick(index, options):
    out = jnp.int32(options[0])
    for n, option in enumerate(options[1:], 1):
        out = jnp.where(index == n, jnp.int32(option), out)
    return out


def kernel(
    q_in, k_in, v_in, text_in, wt_in, px, out_ref,
    raw, stage, kvd, kvs, q_buf, qt_buf, text, wt, part, top, low, ptext, coef, attn, vel, rs, st, st2, ar1, ar2, starts,
    l_in, s_own, r_own, s_blk, s_sib, r_blk, r_sib, s_text, r_text, s_sum, r_sum,
):
    w = lax.axis_index("win")
    s = lax.axis_index("seq")
    x, y = div(w, 8), mod(w, 8)
    p, a = div(y, 2), mod(y, 2)
    z, c = div(s, 2), mod(s, 2)
    base = 8 * x + 2 * p
    block = base + c
    home = 4 * x + p
    head = 2 * z + a
    own_copy = c == a
    zero = jnp.int32(0)

    def dest(d):
        zd, ad = mod(z + div(d, 2), SEQ // 2), mod(a + mod(d, 2), 2)
        return {"win": base + ad, "seq": 2 * zd + a}, 2 * zd + ad

    def source(d):
        return {"win": base + c, "seq": mod(s + d, SEQ)}, mod(s + d, SEQ)

    def along_seq(d):
        return {"win": w, "seq": mod(s + d, SEQ)}

    def along_win(g):
        return {"win": mod(w + g, 32), "seq": s}

    def remote(src, dst, send, recv, to):
        return pltpu.make_async_remote_copy(
            src_ref=src, dst_ref=dst, send_sem=send, recv_sem=recv, device_id=to, device_id_type=MESH
        )

    def await_bytes(ref, sem):
        pltpu.make_async_copy(ref, ref, sem).wait()

    def send_all(copy, keep):
        @pl.when(own_copy)
        def _():
            keep().start()

        @pl.when(jnp.logical_not(own_copy))
        def _():
            copy(zero).start()

        @pl.loop(1, SEQ)
        def _(d):
            copy(d).start()

    sibling = {"win": w, "seq": 2 * z + 1 - c}
    up = {"win": 8 * x + 2 * mod(p + 1, 4) + a, "seq": s}
    down = {"win": 8 * x + 2 * mod(p + 3, 4) + a, "seq": s}
    barrier = pltpu.get_barrier_semaphore()

    def hello(to):
        pl.semaphore_signal(barrier, inc=1, device_id=to, device_id_type=MESH)

    @pl.loop(1, SEQ)
    def _(d):
        hello(source(d)[0])

    @pl.when(jnp.logical_not(own_copy))
    def _():
        hello(source(zero)[0])

    hello(up)
    hello(down)
    hello({"win": 8 * mod(x + 1, 4) + y, "seq": s})
    hello({"win": 8 * mod(x + 3, 4) + y, "seq": s})
    hello(sibling)

    loads = [pltpu.make_async_copy(ref, raw.at[n], l_in.at[n]) for n, ref in enumerate((k_in, v_in, q_in))]
    for load in loads:
        load.start()

    rows = pl.ds(pl.multiple_of(OWN * s, OWN), OWN)
    for n, load in enumerate(loads):
        load.wait()
        flat = raw[n].reshape(OWN, HEADS * HD)
        for h in range(HEADS):
            stage[n, h] = flat[:, h * HD : (h + 1) * HD]
        if n == 0:
            pl.semaphore_wait(barrier, jnp.where(own_copy, SEQ + 4, SEQ + 5))
        dst = q_buf.at[rows, :] if n == 2 else kvd.at[0, n, rows, :]

        def give(d, n=n, dst=dst):
            to, h = dest(d)
            return remote(stage.at[n, h], dst, s_own.at[0], r_own.at[n], to)

        def keep(n=n, dst=dst):
            return pltpu.make_async_copy(stage.at[n, head], dst, r_own.at[n])

        send_all(give, keep)

    def text_sends():
        return (
            remote(text_in, text, s_text.at[0], r_text.at[0], sibling),
            remote(wt_in, wt, s_text.at[1], r_text.at[1], sibling),
        )

    @pl.when(own_copy)
    def _():
        pltpu.make_async_copy(text_in, text, r_text.at[0]).start()
        pltpu.make_async_copy(wt_in, wt, r_text.at[1]).start()
        for copy in text_sends():
            copy.start()

    def place_of(j):
        turn = pick(j, (0, 3, 1, 0, 0, 2, 3, 1, 2))
        pp = mod(p + turn, 4)
        side = jnp.where(j == 3, 1, jnp.where(j == 4, 3, jnp.where(pp < p, 1, 3)))
        far = (j == 3) | (j == 4) | (j >= 6)
        place = pp - p + 4
        place = jnp.where(far, jnp.where(side == 1, place + 4, place - 4), place)
        return place

    def send_block(n, have, step, to):
        remote(kvd.at[have, n], kvd.at[step, n], s_blk.at[0], r_blk.at[step, n], to).start()

    def send_x(n, have, step, side):
        send_block(n, have, step, {"win": 8 * mod(x + side, 4) + y, "seq": s})

    def send_sib(n, step):
        remote(kvd.at[step, n], kvs.at[step, n], s_sib.at[0], r_sib.at[step], sibling).start()

    def hand_on(n, step, turn, x_step):
        await_bytes(kvd.at[step, n], r_blk.at[step, n])
        if step == 1 and n == 0:
            send_block(n, step, 5, up)
        if step == 2 and n == 1:
            send_block(n, step, 5, down)
        send_x(n, step, x_step, jnp.where(mod(p + turn, 4) < p, 3, 1))
        send_sib(n, step)

    await_bytes(kvd.at[0, 0], r_own.at[0])
    send_block(0, 0, 1, up)
    send_x(0, 0, 4, 1)
    send_x(0, 0, 3, 3)
    send_sib(0, 0)
    await_bytes(kvd.at[0, 1], r_own.at[1])
    send_block(1, 0, 2, down)
    send_x(1, 0, 4, 1)
    send_x(1, 0, 3, 3)
    send_sib(1, 0)

    def scan_start(n, found):
        start = div(px[n], 16)
        slot = div(start, 4)
        off = start - 4 * slot
        return tuple(
            old + jnp.where(slot == mod(block + 24 + i, 32), off, 0) for i, old in enumerate(found)
        )

    offsets = lax.fori_loop(0, WINDOWS, scan_start, (zero,) * 9)
    for i in range(9):
        starts[i] = offsets[i]

    await_bytes(q_buf, r_own.at[2])

    qt_buf[...] = q_buf[...].T

    def segment(scores, values_t):
        peak = jnp.maximum(jnp.max(scores, axis=0, keepdims=True), FLOOR)
        weights = jnp.exp2((scores - peak) * SC)
        total = jnp.sum(weights, axis=0, keepdims=True)
        return peak, total, jnp.dot(values_t, weights.astype(bf16), preferred_element_type=f32)

    def attend(held, j, core, place):
        b = 2 * place + core - c
        scores = jnp.dot(held[j, 0], qt_buf[...], preferred_element_type=f32)
        values_t = held[j, 1].T
        key_row = mod(div(lax.broadcasted_iota(jnp.int32, (TOK, 1), 0), 4), 4)

        def keep(kind, masked):
            peak, total, mix = segment(masked, values_t)
            row = b + 1
            top[kind, pl.ds(row, 1), :] = peak
            low[kind, pl.ds(row, 1), :] = total
            part[kind, row] = mix

        keep(0, scores)
        begins = b <= 8
        bound = starts[jnp.clip(jnp.where(begins, b, b - 8), 0, 8)]
        first = jnp.where(begins, bound, 0)
        last = jnp.where(begins, 4, bound)
        inside = (key_row >= first) & (key_row < last)
        keep(1, scores + jnp.where(inside, 0.0, LOW))

        @pl.when(b == 8)
        def _():
            peak, total, mix = segment(scores + jnp.where(key_row < starts[0], 0.0, LOW), values_t)
            top[2, 0:1, :] = peak
            low[2, 0:1, :] = total
            part[2, 0] = mix

    def text_part():
        for n in range(2):
            pltpu.make_async_copy((text_in, wt_in)[n], (text, wt)[n], r_text.at[n]).wait()

        @pl.loop(0, 2)
        def _(branch):
            scores = jnp.dot(text[branch, 0], qt_buf[...], preferred_element_type=f32)
            peak, total, mix = segment(scores, text[branch, 1].T)
            top[2, pl.ds(8 + branch, 1), :] = peak
            low[2, pl.ds(8 + branch, 1), :] = total
            ptext[branch] = mix

    @pl.loop(0, 9)
    def _(j):
        place = place_of(j)

        def pass_on(step):
            for n in range(2):
                await_bytes(kvd.at[step, n], r_blk.at[step, n])
                send_sib(n, step)

        @pl.when(j == 1)
        def _():
            hand_on(0, 1, 3, 6)
            hand_on(1, 2, 1, 7)
            hand_on(1, 1, 3, 6)
            hand_on(0, 2, 1, 7)
            pass_on(3)
            pass_on(4)

        @pl.when(j == 3)
        def _():
            hand_on(0, 5, 2, 8)
            hand_on(1, 5, 2, 8)

        @pl.when(j == 5)
        def _():
            pass_on(6)
            pass_on(7)

        @pl.when(j == 8)
        def _():
            pass_on(8)

        attend(kvd, j, c, place)

        @pl.when(j == 0)
        def _():
            send_block(1, 0, 1, up)
            send_block(0, 0, 2, down)

        @pl.when(j == 0)
        def _():
            text_part()

        await_bytes(kvs.at[j], r_sib.at[j])
        attend(kvs, j, 1 - c, place)

    query_row = mod(div(lax.broadcasted_iota(jnp.int32, (1, TOK), 1), 4), 4)
    holds_first = (query_row < starts[0]).astype(f32)
    holds_last = (query_row >= starts[8]).astype(f32)
    share = 1.0 / (7.0 + holds_first + holds_last)
    which = lax.broadcasted_iota(jnp.int32, (9, TOK), 0)
    member = jnp.where(which == 0, holds_first * share, jnp.where(which == 8, holds_last * share, share))

    head_top, head_low = top[1, 1:10, :], low[1, 1:10, :]
    tail_top = jnp.concatenate([top[2, 0:1, :], top[1, 10:18, :]], axis=0)
    tail_low = jnp.concatenate([low[2, 0:1, :], low[1, 10:18, :]], axis=0)
    peak = jnp.maximum(head_top, tail_top)
    for d in range(1, 8):
        peak = jnp.maximum(peak, top[0, 1 + d : 10 + d, :])
    e_head = jnp.exp2((head_top - peak) * SC)
    e_tail = jnp.exp2((tail_top - peak) * SC)
    total = e_head * head_low + e_tail * tail_low
    e_full = []
    for d in range(1, 8):
        e_full.append(jnp.exp2((top[0, 1 + d : 10 + d, :] - peak) * SC))
        total = total + e_full[-1] * low[0, 1 + d : 10 + d, :]
    coef[...] = jnp.zeros_like(coef)
    for branch in range(2):
        text_top, text_low = top[2, 8 + branch : 9 + branch, :], low[2, 8 + branch : 9 + branch, :]
        both = jnp.maximum(peak, text_top)
        e_img = jnp.exp2((peak - both) * SC)
        e_text = jnp.exp2((text_top - both) * SC)
        scale = member / (e_img * total + e_text * text_low)
        gain = e_img * scale
        for d in range(1, 8):
            coef[branch, 0, 1 + d : 10 + d, :] += gain * e_full[d - 1]
        coef[branch, 1, 1:10, :] = gain * e_head
        coef[branch, 2, 0:9, :] = gain * e_tail
        coef[branch, 2, 9:10, :] = jnp.sum(e_text * scale, axis=0, keepdims=True)

    @pl.loop(0, 8)
    def _(chunk):
        feats = pl.ds(pl.multiple_of(chunk * 16, 16), 16)
        sums = [jnp.zeros((16, TOK), f32), jnp.zeros((16, TOK), f32)]

        def add(value, kind, row):
            for branch in range(2):
                sums[branch] = sums[branch] + value * coef[branch, kind, row : row + 1, :]

        for b in range(1, 16):
            add(part[0, b + 1, feats, :], 0, b + 1)
        for b in range(0, 9):
            add(part[1, b + 1, feats, :], 1, b + 1)
        add(part[2, 0, feats, :], 2, 0)
        for b in range(9, 17):
            add(part[1, b + 1, feats, :], 2, b - 8)
        for branch in range(2):
            mixed = sums[branch] + ptext[branch, feats, :] * coef[branch, 2, 9:10, :]
            main = mixed.astype(bf16)
            attn[pl.ds(pl.multiple_of(branch * HD + chunk * 16, 16), 16), :] = main
            attn[pl.ds(pl.multiple_of((2 + branch) * HD + chunk * 16, 16), 16), :] = (
                mixed - main.astype(f32)
            ).astype(bf16)

    proj = wt[...]
    proj = jnp.concatenate(
        [
            jnp.concatenate([proj, jnp.zeros_like(proj)], axis=1),
            jnp.concatenate([proj, -proj], axis=1),
        ],
        axis=0,
    )
    proj = jnp.concatenate([proj, proj], axis=1)
    vel[...] = jnp.dot(proj, attn[...], preferred_element_type=f32).T.astype(bf16)

    def rs_copy(d):
        to, seq = source(d)
        there = pl.ds(pl.multiple_of(OWN * seq, OWN), OWN)
        return remote(vel.at[there, :], rs.at[head], s_sum.at[0], r_sum.at[0], to)

    send_all(rs_copy, lambda: pltpu.make_async_copy(vel.at[rows, :], rs.at[head], r_sum.at[0]))

    @pl.when(own_copy)
    def _():
        for copy in text_sends():
            copy.wait_send()
        await_bytes(stage.at[:, pl.ds(0, SEQ - 1)], s_own.at[0])
        await_bytes(rs.at[pl.ds(0, SEQ - 1)], s_sum.at[0])

    @pl.when(jnp.logical_not(own_copy))
    def _():
        await_bytes(stage, s_own.at[0])
        await_bytes(rs, s_sum.at[0])

    await_bytes(kvd.at[pl.ds(0, 8)], s_blk.at[0])
    await_bytes(kvd, s_sib.at[0])
    await_bytes(rs, r_sum.at[0])

    mine = jnp.sum(rs[...].astype(f32), axis=0)
    turned = pltpu.roll(mine, LAT, 1)
    st[...] = jnp.concatenate(
        [jnp.sum(mine * mine, axis=0, keepdims=True), jnp.sum(mine * turned, axis=0, keepdims=True)], axis=0
    )

    @pl.loop(1, SEQ)
    def _(d):
        remote(st, ar1.at[s], s_sum.at[1], r_sum.at[1], along_seq(d)).start()

    pltpu.make_async_copy(st, ar1.at[s], r_sum.at[1]).start()
    await_bytes(ar1, r_sum.at[1])
    st2[...] = jnp.sum(ar1[...], axis=0)

    @pl.loop(1, 32)
    def _(g):
        remote(st2, ar2.at[w], s_sum.at[2], r_sum.at[2], along_win(g)).start()

    pltpu.make_async_copy(st2, ar2.at[w], r_sum.at[2]).start()
    await_bytes(ar2, r_sum.at[2])
    sums = jnp.sum(ar2[...], axis=0)
    is_cond = lax.broadcasted_iota(jnp.int32, (1, 2 * LAT), 1) < LAT
    s_cc = jnp.sum(jnp.where(is_cond, sums[0:1, :], 0.0), axis=1, keepdims=True)
    s_dd = jnp.sum(jnp.where(is_cond, 0.0, sums[0:1, :]), axis=1, keepdims=True)
    s_dc = jnp.sum(jnp.where(is_cond, sums[1:2, :], 0.0), axis=1, keepdims=True)
    clip_limit = clip_rms * math.sqrt(ROWS * WIN_COLS * LAT)
    clip_factor = jnp.minimum(1.0, clip_limit / jnp.sqrt(s_dd + tiny))
    along = s_dc / (s_cc + tiny)
    guided = mine + (guide_scale - 1.0) * clip_factor * (turned - along * mine)
    out_ref[...] = guided[:, :LAT]
    await_bytes(ar1.at[pl.ds(0, SEQ - 1)], s_sum.at[1])
    await_bytes(ar2.at[pl.ds(0, 31)], s_sum.at[2])


def local(img_query, img_key, img_value, text_kv, vel_weight, window_px):
    dma = pltpu.SemaphoreType.DMA
    anywhere = pl.BlockSpec(memory_space=pl.ANY)
    out = pl.pallas_call(
        kernel,
        out_shape=jax.ShapeDtypeStruct((OWN, LAT), f32),
        in_specs=[anywhere] * 5 + [pl.BlockSpec(memory_space=pltpu.SMEM)],
        out_specs=pl.BlockSpec(memory_space=pltpu.VMEM),
        scratch_shapes=[
            pltpu.VMEM((3, 4, 4, HEADS * HD), bf16),
            pltpu.VMEM((3, HEADS, OWN, HD), bf16),
            pltpu.VMEM((9, 2, TOK, HD), bf16),
            pltpu.VMEM((9, 2, TOK, HD), bf16),
            pltpu.VMEM((TOK, HD), bf16),
            pltpu.VMEM((HD, TOK), bf16),
            pltpu.VMEM((2, 2, TXT, HD), bf16),
            pltpu.VMEM((LAT, HD), bf16),
            pltpu.VMEM((3, 19, HD, TOK), f32),
            pltpu.VMEM((3, 24, TOK), f32),
            pltpu.VMEM((3, 24, TOK), f32),
            pltpu.VMEM((2, HD, TOK), f32),
            pltpu.VMEM((2, 3, 24, TOK), f32),
            pltpu.VMEM((4 * HD, TOK), bf16),
            pltpu.VMEM((TOK, 2 * LAT), bf16),
            pltpu.VMEM((HEADS, OWN, 2 * LAT), bf16),
            pltpu.VMEM((2, 2 * LAT), f32),
            pltpu.VMEM((2, 2 * LAT), f32),
            pltpu.VMEM((SEQ, 2, 2 * LAT), f32),
            pltpu.VMEM((32, 2, 2 * LAT), f32),
            pltpu.SMEM((9,), jnp.int32),
            dma((3,)),
            dma((1,)),
            dma((3,)),
            dma((1,)),
            dma((1,)),
            dma((9, 2)),
            dma((9,)),
            dma((2,)),
            dma((2,)),
            dma((3,)),
            dma((3,)),
        ],
        compiler_params=pltpu.CompilerParams(
            collective_id=0, has_side_effects=True, vmem_limit_bytes=60 * 2**20
        ),
    )(img_query, img_key, img_value, text_kv, vel_weight.T, window_px)
    return out.reshape(4, 4, LAT)


def solution(mesh):
    in_specs = (
        P("win", "seq", None),
        P("win", "seq", None),
        P("win", "seq", None),
        P(None, None, None, "seq"),
        P("seq", None),
        P(),
    )
    out_specs = P("win", "seq", None)
    return jax.shard_map(local, mesh=mesh, in_specs=in_specs, out_specs=out_specs, check_vma=False)
```

```python
import math

import jax
import jax.numpy as jnp
from jax import lax
from jax.experimental import pallas as pl
from jax.experimental.pallas import tpu as pltpu
from jax.sharding import PartitionSpec as P

HD = 128
HEADS = 16
LAT = 64
TXT = 512
ROWS = 128
WIN_COLS = 64
WINDOWS = 32
SEQ = 16
OWN = 16
TOK = SEQ * OWN

clip_rms = 0.3
guide_scale = 5.0
tiny = 1e-06

SC = math.log2(math.e) / math.sqrt(HD)
LOW = -1e30
FLOOR = -1e29
MESH = pl.DeviceIdType.MESH
f32 = jnp.float32
bf16 = jnp.bfloat16


def mod(value, n):
    return lax.rem(value, jnp.int32(n))


def div(value, n):
    return lax.div(value, jnp.int32(n))


def pick(index, options):
    out = jnp.int32(options[0])
    for n, option in enumerate(options[1:], 1):
        out = jnp.where(index == n, jnp.int32(option), out)
    return out


def kernel(
    q_in, k_in, v_in, text_in, wt_in, px, out_ref,
    raw, stage, kvd, kvs, q_buf, qt_buf, text, wt, part, top, low, ptext, coef, attn, vel, rs, st, st2, ar1, ar2, starts,
    l_in, s_own, r_own, s_blk, s_sib, r_blk, r_sib, s_text, r_text, s_sum, r_sum,
):
    w = lax.axis_index("win")
    s = lax.axis_index("seq")
    x, y = div(w, 8), mod(w, 8)
    p, a = div(y, 2), mod(y, 2)
    z, c = div(s, 2), mod(s, 2)
    base = 8 * x + 2 * p
    block = base + c
    home = 4 * x + p
    head = 2 * z + a
    own_copy = c == a
    zero = jnp.int32(0)

    def dest(d):
        zd, ad = mod(z + div(d, 2), SEQ // 2), mod(a + mod(d, 2), 2)
        return {"win": base + ad, "seq": 2 * zd + a}, 2 * zd + ad

    def source(d):
        return {"win": base + c, "seq": mod(s + d, SEQ)}, mod(s + d, SEQ)

    def along_seq(d):
        return {"win": w, "seq": mod(s + d, SEQ)}

    def along_win(g):
        return {"win": mod(w + g, 32), "seq": s}

    def remote(src, dst, send, recv, to):
        return pltpu.make_async_remote_copy(
            src_ref=src, dst_ref=dst, send_sem=send, recv_sem=recv, device_id=to, device_id_type=MESH
        )

    def await_bytes(ref, sem):
        pltpu.make_async_copy(ref, ref, sem).wait()

    def send_all(copy, keep):
        @pl.when(own_copy)
        def _():
            keep().start()

        @pl.when(jnp.logical_not(own_copy))
        def _():
            copy(zero).start()

        @pl.loop(1, SEQ)
        def _(d):
            copy(d).start()

    sibling = {"win": w, "seq": 2 * z + 1 - c}
    up = {"win": 8 * x + 2 * mod(p + 1, 4) + a, "seq": s}
    down = {"win": 8 * x + 2 * mod(p + 3, 4) + a, "seq": s}
    barrier = pltpu.get_barrier_semaphore()

    def hello(to):
        pl.semaphore_signal(barrier, inc=1, device_id=to, device_id_type=MESH)

    @pl.loop(1, SEQ)
    def _(d):
        hello(source(d)[0])

    @pl.when(jnp.logical_not(own_copy))
    def _():
        hello(source(zero)[0])

    hello(up)
    hello(down)
    hello({"win": 8 * mod(x + 1, 4) + y, "seq": s})
    hello({"win": 8 * mod(x + 3, 4) + y, "seq": s})
    hello(sibling)

    loads = [pltpu.make_async_copy(ref, raw.at[n], l_in.at[n]) for n, ref in enumerate((k_in, v_in, q_in))]
    for load in loads:
        load.start()

    rows = pl.ds(pl.multiple_of(OWN * s, OWN), OWN)
    for n, load in enumerate(loads):
        load.wait()
        flat = raw[n].reshape(OWN, HEADS * HD)
        for h in range(HEADS):
            stage[n, h] = flat[:, h * HD : (h + 1) * HD]
        if n == 0:
            pl.semaphore_wait(barrier, jnp.where(own_copy, SEQ + 4, SEQ + 5))
        dst = q_buf.at[rows, :] if n == 2 else kvd.at[0, n, rows, :]

        def give(d, n=n, dst=dst):
            to, h = dest(d)
            return remote(stage.at[n, h], dst, s_own.at[0], r_own.at[n], to)

        def keep(n=n, dst=dst):
            return pltpu.make_async_copy(stage.at[n, head], dst, r_own.at[n])

        send_all(give, keep)

    def text_sends():
        return (
            remote(text_in, text, s_text.at[0], r_text.at[0], sibling),
            remote(wt_in, wt, s_text.at[1], r_text.at[1], sibling),
        )

    @pl.when(own_copy)
    def _():
        pltpu.make_async_copy(text_in, text, r_text.at[0]).start()
        pltpu.make_async_copy(wt_in, wt, r_text.at[1]).start()
        for copy in text_sends():
            copy.start()

    def place_of(j):
        turn = pick(j, (0, 3, 1, 0, 0, 2, 3, 1, 2))
        pp = mod(p + turn, 4)
        side = jnp.where(j == 3, 1, jnp.where(j == 4, 3, jnp.where(pp < p, 1, 3)))
        far = (j == 3) | (j == 4) | (j >= 6)
        place = pp - p + 4
        place = jnp.where(far, jnp.where(side == 1, place + 4, place - 4), place)
        return place

    def send_block(n, have, step, to):
        remote(kvd.at[have, n], kvd.at[step, n], s_blk.at[0], r_blk.at[step, n], to).start()

    def send_x(n, have, step, side):
        send_block(n, have, step, {"win": 8 * mod(x + side, 4) + y, "seq": s})

    def send_sib(n, step):
        remote(kvd.at[step, n], kvs.at[step, n], s_sib.at[0], r_sib.at[step], sibling).start()

    def hand_on(n, step, turn, x_step):
        await_bytes(kvd.at[step, n], r_blk.at[step, n])
        if step == 1 and n == 0:
            send_block(n, step, 5, up)
        if step == 2 and n == 1:
            send_block(n, step, 5, down)
        send_x(n, step, x_step, jnp.where(mod(p + turn, 4) < p, 3, 1))
        send_sib(n, step)

    await_bytes(kvd.at[0, 0], r_own.at[0])
    send_block(0, 0, 1, up)
    send_x(0, 0, 4, 1)
    send_x(0, 0, 3, 3)
    await_bytes(kvd.at[0, 1], r_own.at[1])
    send_block(1, 0, 2, down)
    send_x(1, 0, 4, 1)
    send_x(1, 0, 3, 3)
    send_sib(0, 0)
    send_sib(1, 0)

    def scan_start(n, found):
        start = div(px[n], 16)
        slot = div(start, 4)
        off = start - 4 * slot
        return tuple(
            old + jnp.where(slot == mod(block + 24 + i, 32), off, 0) for i, old in enumerate(found)
        )

    offsets = lax.fori_loop(0, WINDOWS, scan_start, (zero,) * 9)
    for i in range(9):
        starts[i] = offsets[i]

    await_bytes(q_buf, r_own.at[2])

    qt_buf[...] = q_buf[...].T

    def segment(scores, values_t):
        peak = jnp.maximum(jnp.max(scores, axis=0, keepdims=True), FLOOR)
        weights = jnp.exp2((scores - peak) * SC)
        total = jnp.sum(weights, axis=0, keepdims=True)
        return peak, total, jnp.dot(values_t, weights.astype(bf16), preferred_element_type=f32)

    def attend(held, j, core, place):
        b = 2 * place + core - c
        scores = jnp.dot(held[j, 0], qt_buf[...], preferred_element_type=f32)
        values_t = held[j, 1].T
        key_row = mod(div(lax.broadcasted_iota(jnp.int32, (TOK, 1), 0), 4), 4)

        def keep(kind, masked):
            peak, total, mix = segment(masked, values_t)
            row = b + 1
            top[kind, pl.ds(row, 1), :] = peak
            low[kind, pl.ds(row, 1), :] = total
            part[kind, row] = mix

        keep(0, scores)
        begins = b <= 8
        bound = starts[jnp.clip(jnp.where(begins, b, b - 8), 0, 8)]
        first = jnp.where(begins, bound, 0)
        last = jnp.where(begins, 4, bound)
        inside = (key_row >= first) & (key_row < last)
        keep(1, scores + jnp.where(inside, 0.0, LOW))

        @pl.when(b == 8)
        def _():
            peak, total, mix = segment(scores + jnp.where(key_row < starts[0], 0.0, LOW), values_t)
            top[2, 0:1, :] = peak
            low[2, 0:1, :] = total
            part[2, 0] = mix

    def text_part():
        for n in range(2):
            pltpu.make_async_copy((text_in, wt_in)[n], (text, wt)[n], r_text.at[n]).wait()

        @pl.loop(0, 2)
        def _(branch):
            scores = jnp.dot(text[branch, 0], qt_buf[...], preferred_element_type=f32)
            peak, total, mix = segment(scores, text[branch, 1].T)
            top[2, pl.ds(8 + branch, 1), :] = peak
            low[2, pl.ds(8 + branch, 1), :] = total
            ptext[branch] = mix

    @pl.loop(0, 9)
    def _(j):
        place = place_of(j)

        def pass_on(step):
            for n in range(2):
                await_bytes(kvd.at[step, n], r_blk.at[step, n])
                send_sib(n, step)

        @pl.when(j == 1)
        def _():
            hand_on(0, 1, 3, 6)
            hand_on(1, 2, 1, 7)
            hand_on(1, 1, 3, 6)
            hand_on(0, 2, 1, 7)
            pass_on(3)
            pass_on(4)

        @pl.when(j == 3)
        def _():
            hand_on(0, 5, 2, 8)
            hand_on(1, 5, 2, 8)

        @pl.when(j == 5)
        def _():
            pass_on(6)
            pass_on(7)

        @pl.when(j == 8)
        def _():
            pass_on(8)

        attend(kvd, j, c, place)

        @pl.when(j == 0)
        def _():
            send_block(1, 0, 1, up)
            send_block(0, 0, 2, down)

        @pl.when(j == 0)
        def _():
            text_part()

        await_bytes(kvs.at[j], r_sib.at[j])
        attend(kvs, j, 1 - c, place)

    query_row = mod(div(lax.broadcasted_iota(jnp.int32, (1, TOK), 1), 4), 4)
    holds_first = (query_row < starts[0]).astype(f32)
    holds_last = (query_row >= starts[8]).astype(f32)
    share = 1.0 / (7.0 + holds_first + holds_last)
    which = lax.broadcasted_iota(jnp.int32, (9, TOK), 0)
    member = jnp.where(which == 0, holds_first * share, jnp.where(which == 8, holds_last * share, share))

    head_top, head_low = top[1, 1:10, :], low[1, 1:10, :]
    tail_top = jnp.concatenate([top[2, 0:1, :], top[1, 10:18, :]], axis=0)
    tail_low = jnp.concatenate([low[2, 0:1, :], low[1, 10:18, :]], axis=0)
    peak = jnp.maximum(head_top, tail_top)
    for d in range(1, 8):
        peak = jnp.maximum(peak, top[0, 1 + d : 10 + d, :])
    e_head = jnp.exp2((head_top - peak) * SC)
    e_tail = jnp.exp2((tail_top - peak) * SC)
    total = e_head * head_low + e_tail * tail_low
    e_full = []
    for d in range(1, 8):
        e_full.append(jnp.exp2((top[0, 1 + d : 10 + d, :] - peak) * SC))
        total = total + e_full[-1] * low[0, 1 + d : 10 + d, :]
    coef[...] = jnp.zeros_like(coef)
    for branch in range(2):
        text_top, text_low = top[2, 8 + branch : 9 + branch, :], low[2, 8 + branch : 9 + branch, :]
        both = jnp.maximum(peak, text_top)
        e_img = jnp.exp2((peak - both) * SC)
        e_text = jnp.exp2((text_top - both) * SC)
        scale = member / (e_img * total + e_text * text_low)
        gain = e_img * scale
        for d in range(1, 8):
            coef[branch, 0, 1 + d : 10 + d, :] += gain * e_full[d - 1]
        coef[branch, 1, 1:10, :] = gain * e_head
        coef[branch, 2, 0:9, :] = gain * e_tail
        coef[branch, 2, 9:10, :] = jnp.sum(e_text * scale, axis=0, keepdims=True)

    @pl.loop(0, 8)
    def _(chunk):
        feats = pl.ds(pl.multiple_of(chunk * 16, 16), 16)
        sums = [jnp.zeros((16, TOK), f32), jnp.zeros((16, TOK), f32)]

        def add(value, kind, row):
            for branch in range(2):
                sums[branch] = sums[branch] + value * coef[branch, kind, row : row + 1, :]

        for b in range(1, 16):
            add(part[0, b + 1, feats, :], 0, b + 1)
        for b in range(0, 9):
            add(part[1, b + 1, feats, :], 1, b + 1)
        add(part[2, 0, feats, :], 2, 0)
        for b in range(9, 17):
            add(part[1, b + 1, feats, :], 2, b - 8)
        for branch in range(2):
            mixed = sums[branch] + ptext[branch, feats, :] * coef[branch, 2, 9:10, :]
            main = mixed.astype(bf16)
            attn[pl.ds(pl.multiple_of(branch * HD + chunk * 16, 16), 16), :] = main
            attn[pl.ds(pl.multiple_of((2 + branch) * HD + chunk * 16, 16), 16), :] = (
                mixed - main.astype(f32)
            ).astype(bf16)

    proj = wt[...]
    proj = jnp.concatenate(
        [
            jnp.concatenate([proj, jnp.zeros_like(proj)], axis=1),
            jnp.concatenate([proj, -proj], axis=1),
        ],
        axis=0,
    )
    proj = jnp.concatenate([proj, proj], axis=1)
    vel[...] = jnp.dot(proj, attn[...], preferred_element_type=f32).T.astype(bf16)

    def rs_copy(d):
        to, seq = source(d)
        there = pl.ds(pl.multiple_of(OWN * seq, OWN), OWN)
        return remote(vel.at[there, :], rs.at[head], s_sum.at[0], r_sum.at[0], to)

    send_all(rs_copy, lambda: pltpu.make_async_copy(vel.at[rows, :], rs.at[head], r_sum.at[0]))

    @pl.when(own_copy)
    def _():
        for copy in text_sends():
            copy.wait_send()
        await_bytes(stage.at[:, pl.ds(0, SEQ - 1)], s_own.at[0])
        await_bytes(rs.at[pl.ds(0, SEQ - 1)], s_sum.at[0])

    @pl.when(jnp.logical_not(own_copy))
    def _():
        await_bytes(stage, s_own.at[0])
        await_bytes(rs, s_sum.at[0])

    await_bytes(kvd.at[pl.ds(0, 8)], s_blk.at[0])
    await_bytes(kvd, s_sib.at[0])
    await_bytes(rs, r_sum.at[0])

    mine = jnp.sum(rs[...].astype(f32), axis=0)
    turned = pltpu.roll(mine, LAT, 1)
    st[...] = jnp.concatenate(
        [jnp.sum(mine * mine, axis=0, keepdims=True), jnp.sum(mine * turned, axis=0, keepdims=True)], axis=0
    )

    @pl.loop(1, SEQ)
    def _(d):
        remote(st, ar1.at[s], s_sum.at[1], r_sum.at[1], along_seq(d)).start()

    pltpu.make_async_copy(st, ar1.at[s], r_sum.at[1]).start()
    await_bytes(ar1, r_sum.at[1])
    st2[...] = jnp.sum(ar1[...], axis=0)

    @pl.loop(1, 32)
    def _(g):
        remote(st2, ar2.at[w], s_sum.at[2], r_sum.at[2], along_win(g)).start()

    pltpu.make_async_copy(st2, ar2.at[w], r_sum.at[2]).start()
    await_bytes(ar2, r_sum.at[2])
    sums = jnp.sum(ar2[...], axis=0)
    is_cond = lax.broadcasted_iota(jnp.int32, (1, 2 * LAT), 1) < LAT
    s_cc = jnp.sum(jnp.where(is_cond, sums[0:1, :], 0.0), axis=1, keepdims=True)
    s_dd = jnp.sum(jnp.where(is_cond, 0.0, sums[0:1, :]), axis=1, keepdims=True)
    s_dc = jnp.sum(jnp.where(is_cond, sums[1:2, :], 0.0), axis=1, keepdims=True)
    clip_limit = clip_rms * math.sqrt(ROWS * WIN_COLS * LAT)
    clip_factor = jnp.minimum(1.0, clip_limit / jnp.sqrt(s_dd + tiny))
    along = s_dc / (s_cc + tiny)
    guided = mine + (guide_scale - 1.0) * clip_factor * (turned - along * mine)
    out_ref[...] = guided[:, :LAT]
    await_bytes(ar1.at[pl.ds(0, SEQ - 1)], s_sum.at[1])
    await_bytes(ar2.at[pl.ds(0, 31)], s_sum.at[2])


def local(img_query, img_key, img_value, text_kv, vel_weight, window_px):
    dma = pltpu.SemaphoreType.DMA
    anywhere = pl.BlockSpec(memory_space=pl.ANY)
    out = pl.pallas_call(
        kernel,
        out_shape=jax.ShapeDtypeStruct((OWN, LAT), f32),
        in_specs=[anywhere] * 5 + [pl.BlockSpec(memory_space=pltpu.SMEM)],
        out_specs=pl.BlockSpec(memory_space=pltpu.VMEM),
        scratch_shapes=[
            pltpu.VMEM((3, 4, 4, HEADS * HD), bf16),
            pltpu.VMEM((3, HEADS, OWN, HD), bf16),
            pltpu.VMEM((9, 2, TOK, HD), bf16),
            pltpu.VMEM((9, 2, TOK, HD), bf16),
            pltpu.VMEM((TOK, HD), bf16),
            pltpu.VMEM((HD, TOK), bf16),
            pltpu.VMEM((2, 2, TXT, HD), bf16),
            pltpu.VMEM((LAT, HD), bf16),
            pltpu.VMEM((3, 19, HD, TOK), f32),
            pltpu.VMEM((3, 24, TOK), f32),
            pltpu.VMEM((3, 24, TOK), f32),
            pltpu.VMEM((2, HD, TOK), f32),
            pltpu.VMEM((2, 3, 24, TOK), f32),
            pltpu.VMEM((4 * HD, TOK), bf16),
            pltpu.VMEM((TOK, 2 * LAT), bf16),
            pltpu.VMEM((HEADS, OWN, 2 * LAT), bf16),
            pltpu.VMEM((2, 2 * LAT), f32),
            pltpu.VMEM((2, 2 * LAT), f32),
            pltpu.VMEM((SEQ, 2, 2 * LAT), f32),
            pltpu.VMEM((32, 2, 2 * LAT), f32),
            pltpu.SMEM((9,), jnp.int32),
            dma((3,)),
            dma((1,)),
            dma((3,)),
            dma((1,)),
            dma((1,)),
            dma((9, 2)),
            dma((9,)),
            dma((2,)),
            dma((2,)),
            dma((3,)),
            dma((3,)),
        ],
        compiler_params=pltpu.CompilerParams(
            collective_id=0, has_side_effects=True, vmem_limit_bytes=60 * 2**20
        ),
    )(img_query, img_key, img_value, text_kv, vel_weight.T, window_px)
    return out.reshape(4, 4, LAT)


def solution(mesh):
    in_specs = (
        P("win", "seq", None),
        P("win", "seq", None),
        P("win", "seq", None),
        P(None, None, None, "seq"),
        P("seq", None),
        P(),
    )
    out_specs = P("win", "seq", None)
    return jax.shard_map(local, mesh=mesh, in_specs=in_specs, out_specs=out_specs, check_vma=False)
```
